32 devices in a mesh: hours: 2 (over x), chan: 2 (over core), freq: 8 (over z, y).
Axes of the slice: x: 2, y: 2, z: 4, core: 2. Of those that a mesh axis runs over, the one named last changes fastest.
Arguments:
- samples: bfloat16 [1152, 32, 1024], P('chan', ('hours', 'freq')), parts along dimension 1, may hold values from -18 to 18
Outputs:
- cross_spectra: bfloat16 [2, 256, 1152, 1152], P(None, ('hours', 'freq'), None, 'chan'), parts along dimension 1
The draws below stay inside these ranges and needn't reach their ends.
There are 2 independent parts, one for each index of `hours`. The reference program is written for one: setup_inputs(seed, part) draws one part's arguments, and reference() takes and returns one part's arrays. A program takes and returns all parts, laid end to end along the dimension named above; each array names one. Nothing has to cross between parts.
All inputs are finite; a program needn't handle non-finite values.
Results may differ from the reference program's by a relative error of at most 0.008.
Values may be sent and summed in bfloat16 or wider, within the bound.
A program may use at most 192 MiB of HBM per device.

```python
import math
import jax
import jax.numpy as jnp
from jax import lax

CHANNELS = 1152
SAMPLES = 1024
BINS = 128
WINDOWS = 16


def draw_samples(key, part):
    first, second = jax.random.split(jax.random.fold_in(key, 7), 2)
    gains = jnp.exp(jax.random.uniform(first, (CHANNELS, 1, 1), jnp.float32, math.log(0.1), math.log(3.0)))
    values = jnp.clip(jax.random.normal(second, (CHANNELS, WINDOWS, SAMPLES), jnp.float32), -6.0, 6.0)
    return (gains * values).astype(jnp.bfloat16)


def setup_inputs(seed: int = 0, part: int = 0) -> dict:
    arg_keys = jax.random.split(jax.random.key(seed), 2)
    part_keys = jax.random.split(jax.random.fold_in(arg_keys[1], part), 2)
    samples = draw_samples(jax.random.fold_in(jax.random.fold_in(arg_keys[1], part), 71), part)
    return dict(samples=samples)


def bin_table(length, bins):
    position = lax.broadcasted_iota(jnp.int32, (length, bins), 0)
    number = lax.broadcasted_iota(jnp.int32, (length, bins), 1) + 1
    phase = (position * number % length).astype(jnp.float32) * (2.0 * math.pi / length)
    taper = 0.5 - 0.5 * jnp.cos(position.astype(jnp.float32) * (2.0 * math.pi / length))
    factor = math.sqrt(8.0 / (3.0 * length))
    table = jnp.concatenate([taper * jnp.cos(phase), -(taper * jnp.sin(phase))], axis=1) * factor
    return table.astype(jnp.bfloat16)

def whiten(padded, first_bin, total_bins):
    count_bins = padded.shape[1] - 4
    values = padded.astype(jnp.float32)
    power = values[0] * values[0] + values[1] * values[1]
    summed = power[0:count_bins] + power[1:count_bins + 1]
    summed = summed + power[2:count_bins + 2]
    summed = summed + power[3:count_bins + 3]
    summed = summed + power[4:count_bins + 4]
    which = first_bin + jnp.arange(count_bins, dtype=jnp.int32)
    upper = jnp.minimum(which + 2, total_bins - 1)
    lower = jnp.maximum(which - 2, 0)
    count = (upper - lower + 1).astype(jnp.float32)
    level = jnp.maximum(summed / count[:, None, None], 0.1)
    return (values[:, 2:count_bins + 2] / jnp.sqrt(level)[None]).astype(jnp.bfloat16)

def reference(samples):
    channels, windows, length = samples.shape
    table = bin_table(length, BINS)
    flat = jnp.dot(samples.reshape(channels * windows, length), table, preferred_element_type=jnp.float32)
    spectrum = flat.reshape(channels, windows, 2, BINS).transpose(2, 3, 1, 0).astype(jnp.bfloat16)
    padded = jnp.pad(spectrum, ((0, 0), (2, 2), (0, 0), (0, 0)))
    whitened = whiten(padded, 0, BINS)

    def one_bin(index):
        single = lax.dynamic_index_in_dim(whitened, index, 1, keepdims=False).astype(jnp.float32)
        real_part = jnp.einsum('pwa,pwb->ab', single, single)
        rotated = jnp.stack([-single[1], single[0]])
        imag_part = jnp.einsum('pwa,pwb->ab', single, rotated)
        return (jnp.stack([real_part, imag_part]) / windows).astype(jnp.bfloat16)
    stacked = lax.map(one_bin, jnp.arange(BINS, dtype=jnp.int32))
    return jnp.transpose(stacked, (1, 0, 3, 2))
```

```python
import functools
import math

import jax
import jax.numpy as jnp
import numpy as np
from jax import lax
from jax.experimental import pallas as pl
from jax.experimental.pallas import tpu as pltpu
from jax.sharding import PartitionSpec as P

BINS = 128
LANES = 128
MESH = pl.DeviceIdType.MESH


def bin_table(length, bins):
    position = np.arange(length, dtype=np.int64)[:, None]
    number = np.arange(bins, dtype=np.int64)[None, :] + 1
    step = np.float32(2.0 * math.pi / length)
    phase = (position * number % length).astype(np.float32) * step
    half = np.float32(0.5)
    taper = half - half * np.cos(position.astype(np.float32) * step)
    factor = np.float32(math.sqrt(8.0 / (3.0 * length)))
    table = np.concatenate([taper * np.cos(phase), -(taper * np.sin(phase))], axis=1) * factor
    return jnp.asarray(table.astype(np.float32)).astype(jnp.bfloat16)


def whiten(real, imag):
    bins = real.shape[0]
    power = real * real + imag * imag
    row = lax.broadcasted_iota(jnp.int32, (bins, 1), 0)
    summed = power
    for shift in (1, 2):
        summed = summed + jnp.where(row >= shift, pltpu.roll(power, shift, 0), 0.0)
        summed = summed + jnp.where(row < bins - shift, pltpu.roll(power, bins - shift, 0), 0.0)
    count = jnp.minimum(row + 2, bins - 1) - jnp.maximum(row - 2, 0) + 1
    level = jnp.maximum(summed * (1.0 / count.astype(jnp.float32)), 0.1)
    scale = lax.rsqrt(level)
    return (real * scale).astype(jnp.bfloat16), (imag * scale).astype(jnp.bfloat16)


def exchange_kernel(count, spec_ref, own_ref, other_ref, white, send_sem, recv_sem, local_sem,
                    pass_sem, got_sem):
    hour = lax.axis_index("hours")
    chan = lax.axis_index("chan")
    me = lax.axis_index("freq")
    windows, _, _ = spec_ref.shape
    local_bins = own_ref.shape[2]
    peers = [lax.rem(me + step, count) for step in range(1, count)]

    barrier = pltpu.get_barrier_semaphore()
    for peer in peers:
        pl.semaphore_signal(barrier, inc=1, device_id=(hour, chan, peer), device_id_type=MESH)
    pl.semaphore_signal(barrier, inc=1, device_id=(hour, 1 - chan, me), device_id_type=MESH)

    for w in range(windows):
        turned = spec_ref[w].astype(jnp.float32).T
        real, imag = whiten(turned[:BINS], turned[BINS:])
        white[0, w] = real.reshape(count, local_bins, real.shape[1])
        white[1, w] = imag.reshape(count, local_bins, imag.shape[1])

    pl.semaphore_wait(barrier, count)

    mine = pl.ds(windows * me, windows)
    copies = []
    for step in range(1, count):
        copy = pltpu.make_async_remote_copy(
            src_ref=white.at[:, :, peers[step - 1]],
            dst_ref=own_ref.at[:, mine],
            send_sem=send_sem.at[step],
            recv_sem=recv_sem.at[step],
            device_id=(hour, chan, peers[step - 1]),
            device_id_type=MESH,
        )
        copy.start()
        copies.append(copy)
    keep = pltpu.make_async_copy(white.at[:, :, me], own_ref.at[:, mine], local_sem)
    keep.start()
    passes = []

    def forward(source_ref, owner, slot):
        part = pl.ds(windows * owner, windows)
        copy = pltpu.make_async_remote_copy(
            src_ref=source_ref,
            dst_ref=other_ref.at[:, part],
            send_sem=pass_sem.at[slot],
            recv_sem=got_sem.at[slot],
            device_id=(hour, 1 - chan, me),
            device_id_type=MESH,
        )
        copy.start()
        passes.append(copy)

    forward(white.at[:, :, me], me, 0)
    for step in range(1, count):
        copies[step - 1].wait_recv()
        owner = lax.rem(me - step + count, count)
        forward(own_ref.at[:, pl.ds(windows * owner, windows)], owner, step)
    keep.wait()
    for copy in copies:
        copy.wait_send()
    for copy in passes:
        copy.wait()


def exchange(spec, count):
    windows, channels, _ = spec.shape
    local_bins = BINS // count
    shape = jax.ShapeDtypeStruct((2, windows * count, local_bins, channels), jnp.bfloat16)
    size = spec.size * 2
    return pl.pallas_call(
        functools.partial(exchange_kernel, count),
        out_shape=(shape, shape),
        in_specs=[pl.BlockSpec(memory_space=pltpu.VMEM)],
        out_specs=(pl.BlockSpec(memory_space=pl.ANY), pl.BlockSpec(memory_space=pl.ANY)),
        scratch_shapes=[
            pltpu.VMEM((2, windows, count, local_bins, channels), jnp.bfloat16),
            pltpu.SemaphoreType.DMA((count,)),
            pltpu.SemaphoreType.DMA((count,)),
            pltpu.SemaphoreType.DMA,
            pltpu.SemaphoreType.DMA((count,)),
            pltpu.SemaphoreType.DMA((count,)),
        ],
        compiler_params=pltpu.CompilerParams(
            collective_id=0, has_side_effects=True, vmem_limit_bytes=40 << 20
        ),
        cost_estimate=pl.CostEstimate(flops=spec.size * 20, bytes_accessed=size * 4, transcendentals=0),
        name="exchange",
    )(spec)


def spread(tiles, values):
    width = values.shape[1]
    for t in range(tiles.shape[0]):
        part = values[:, t * LANES : min((t + 1) * LANES, width)]
        if part.shape[1] < LANES:
            part = jnp.concatenate(
                [part, jnp.zeros((part.shape[0], LANES - part.shape[1]), part.dtype)], axis=1
            )
        tiles[t] = part


def cross_kernel(scale, own_ref, other_ref, out_ref, mine, every):
    chan = lax.axis_index("chan")
    parts, windows, local_bins, channels = own_ref.shape
    rows = parts * windows * local_bins
    k = pl.program_id(0)

    @pl.when(k == 0)
    def _():
        own = own_ref[...].astype(jnp.float32).reshape(rows, channels)
        other = other_ref[...].astype(jnp.float32).reshape(rows, channels)
        spread(mine, own)
        first = jnp.where(chan == 0, own, other)
        second = jnp.where(chan == 0, other, own)
        spread(every, jnp.concatenate([first, second], axis=1))

    pick = pl.ds(k, parts * windows, stride=local_bins)
    here = jnp.concatenate([mine[t, pick, :] for t in range(mine.shape[0])], axis=1)[:, :channels]
    left = here.astype(jnp.bfloat16)
    swapped = jnp.concatenate([here[windows:], -here[:windows]], axis=0).astype(jnp.bfloat16)
    right = jnp.concatenate(
        [every[t, pick, :].astype(jnp.bfloat16) for t in range(every.shape[0])], axis=1
    )[:, : 2 * channels]
    for part, side in ((0, left), (1, swapped)):
        product = lax.dot_general(
            side, right, (((0,), (0,)), ((), ())), preferred_element_type=jnp.float32
        )
        out_ref[part, 0] = (product * scale).astype(jnp.bfloat16)


def cross(own, other):
    parts, windows, local_bins, channels = own.shape
    rows = parts * windows * local_bins
    shape = (parts, local_bins, channels, 2 * channels)
    whole = pl.BlockSpec(memory_space=pltpu.VMEM)
    return pl.pallas_call(
        functools.partial(cross_kernel, 1.0 / windows),
        grid=(local_bins,),
        out_shape=jax.ShapeDtypeStruct(shape, jnp.bfloat16),
        in_specs=[whole, whole],
        out_specs=pl.BlockSpec((parts, 1, channels, 2 * channels), lambda k: (0, k, 0, 0)),
        scratch_shapes=[
            pltpu.VMEM((pl.cdiv(channels, LANES), rows, LANES), jnp.float32),
            pltpu.VMEM((pl.cdiv(2 * channels, LANES), rows, LANES), jnp.float32),
        ],
        compiler_params=pltpu.CompilerParams(vmem_limit_bytes=50 << 20),
        cost_estimate=pl.CostEstimate(
            flops=2 * rows * channels * 2 * channels * 2,
            bytes_accessed=2 * math.prod(shape),
            transcendentals=0,
        ),
        name="cross",
    )(own, other)


def local(samples):
    length = samples.shape[2]
    table = bin_table(length, BINS)
    spec = jnp.einsum("cws,sj->wcj", samples, table, preferred_element_type=jnp.float32)
    own, other = exchange(spec.astype(jnp.bfloat16), lax.axis_size("freq"))
    return jnp.swapaxes(cross(own, other), 2, 3)


def solution(mesh):
    return jax.shard_map(
        local,
        mesh=mesh,
        in_specs=(P("chan", ("hours", "freq"), None),),
        out_specs=P(None, ("hours", "freq"), None, "chan"),
        check_vma=False,
    )
```

```python
import functools
import math

import jax
import jax.numpy as jnp
import numpy as np
from jax import lax
from jax.experimental import pallas as pl
from jax.experimental.pallas import tpu as pltpu
from jax.sharding import PartitionSpec as P

BINS = 128
LANES = 128
MESH = pl.DeviceIdType.MESH


def bin_table(length, bins):
    position = np.arange(length, dtype=np.int64)[:, None]
    number = np.arange(bins, dtype=np.int64)[None, :] + 1
    step = np.float32(2.0 * math.pi / length)
    phase = (position * number % length).astype(np.float32) * step
    half = np.float32(0.5)
    taper = half - half * np.cos(position.astype(np.float32) * step)
    factor = np.float32(math.sqrt(8.0 / (3.0 * length)))
    table = np.concatenate([taper * np.cos(phase), -(taper * np.sin(phase))], axis=1) * factor
    return jnp.asarray(table.astype(np.float32)).astype(jnp.bfloat16)


def whiten(real, imag):
    bins = real.shape[0]
    power = real * real + imag * imag
    row = lax.broadcasted_iota(jnp.int32, (bins, 1), 0)
    summed = power
    for shift in (1, 2):
        summed = summed + jnp.where(row >= shift, pltpu.roll(power, shift, 0), 0.0)
        summed = summed + jnp.where(row < bins - shift, pltpu.roll(power, bins - shift, 0), 0.0)
    count = jnp.minimum(row + 2, bins - 1) - jnp.maximum(row - 2, 0) + 1
    level = jnp.maximum(summed * (1.0 / count.astype(jnp.float32)), 0.1)
    scale = lax.rsqrt(level)
    return real * scale, imag * scale


def pack(real, imag):
    cut = real.shape[1] // LANES * LANES
    return jnp.concatenate([real[:, :cut], imag[:, :cut], real[:, cut:], imag[:, cut:]], axis=1)


def unpack(values, part, channels):
    cut = channels // LANES * LANES
    rest = channels - cut
    tail = 2 * cut + part * rest
    main = values[:, part * cut : (part + 1) * cut]
    return jnp.concatenate([main, values[:, tail : tail + rest]], axis=1) if rest else main


def exchange_kernel(count, spec_ref, own_ref, other_ref, white, send_sem, recv_sem, local_sem,
                    pass_sem, got_sem):
    hour = lax.axis_index("hours")
    chan = lax.axis_index("chan")
    me = lax.axis_index("freq")
    windows = spec_ref.shape[0]
    local_bins, width = own_ref.shape[1:]
    steps = sorted(range(1, count), key=lambda step: abs(2 * step - count))

    barrier = pltpu.get_barrier_semaphore()
    for step in steps:
        peer = lax.rem(me + step, count)
        pl.semaphore_signal(barrier, inc=1, device_id=(hour, chan, peer), device_id_type=MESH)
    pl.semaphore_signal(barrier, inc=1, device_id=(hour, 1 - chan, me), device_id_type=MESH)

    copies, keeps, passes = {}, [], []

    def forward(source_ref, owner, w, step):
        slot = w * count + step
        copy = pltpu.make_async_remote_copy(
            src_ref=source_ref,
            dst_ref=other_ref.at[windows * owner + w],
            send_sem=pass_sem.at[slot],
            recv_sem=got_sem.at[slot],
            device_id=(hour, 1 - chan, me),
            device_id_type=MESH,
        )
        copy.start()
        passes.append(copy)

    for w in range(windows):
        turned = spec_ref[w].astype(jnp.float32).T
        real, imag = whiten(turned[:BINS], turned[BINS:])
        packed = pack(real, imag).astype(jnp.bfloat16)
        white[w] = packed.reshape(count, local_bins, width)
        if w == 0:
            pl.semaphore_wait(barrier, count)
        for step in steps:
            peer = lax.rem(me + step, count)
            copy = pltpu.make_async_remote_copy(
                src_ref=white.at[w, peer],
                dst_ref=own_ref.at[windows * me + w],
                send_sem=send_sem.at[w * count + step],
                recv_sem=recv_sem.at[w * count + step],
                device_id=(hour, chan, peer),
                device_id_type=MESH,
            )
            copy.start()
            copies[w, step] = copy
    for w in range(windows):
        keep = pltpu.make_async_copy(white.at[w, me], own_ref.at[windows * me + w], local_sem.at[w])
        keep.start()
        keeps.append(keep)
        forward(white.at[w, me], me, w, 0)
    for w in range(windows):
        for step in reversed(steps):
            copies[w, step].wait_recv()
            owner = lax.rem(me - step + count, count)
            forward(own_ref.at[windows * owner + w], owner, w, step)
    for keep in keeps:
        keep.wait()
    for copy in copies.values():
        copy.wait_send()
    for copy in passes:
        copy.wait()


def exchange(spec, count):
    windows, channels, _ = spec.shape
    local_bins = BINS // count
    shape = jax.ShapeDtypeStruct((windows * count, local_bins, 2 * channels), jnp.bfloat16)
    pieces = pltpu.SemaphoreType.DMA((windows * count,))
    return pl.pallas_call(
        functools.partial(exchange_kernel, count),
        out_shape=(shape, shape),
        in_specs=[pl.BlockSpec(memory_space=pltpu.VMEM)],
        out_specs=(pl.BlockSpec(memory_space=pl.ANY), pl.BlockSpec(memory_space=pl.ANY)),
        scratch_shapes=[
            pltpu.VMEM((windows, count, local_bins, 2 * channels), jnp.bfloat16),
            pieces,
            pieces,
            pltpu.SemaphoreType.DMA((windows,)),
            pieces,
            pieces,
        ],
        compiler_params=pltpu.CompilerParams(
            collective_id=0, has_side_effects=True, vmem_limit_bytes=40 << 20
        ),
        cost_estimate=pl.CostEstimate(
            flops=spec.size * 20, bytes_accessed=spec.size * 8, transcendentals=0
        ),
        name="exchange",
    )(spec)


def spread(tiles, first_row, values):
    height, width = values.shape
    for t in range(tiles.shape[0]):
        part = values[:, t * LANES : min((t + 1) * LANES, width)]
        if part.shape[1] < LANES:
            gap = jnp.zeros((height, LANES - part.shape[1]), part.dtype)
            part = jnp.concatenate([part, gap], axis=1)
        tiles[t, first_row : first_row + height] = part


def cross_kernel(scale, own_ref, other_ref, out_ref, mine, every):
    chan = lax.axis_index("chan")
    windows, local_bins, width = own_ref.shape
    channels = width // 2
    rows = windows * local_bins
    step_bins = out_ref.shape[1]
    step = pl.program_id(0)

    @pl.when(step == 0)
    def _():
        own = own_ref[...].astype(jnp.float32).reshape(rows, width)
        other = other_ref[...].astype(jnp.float32).reshape(rows, width)
        first = jnp.where(chan == 0, own, other)
        second = jnp.where(chan == 0, other, own)
        for part in range(2):
            spread(mine, part * rows, unpack(own, part, channels))
            pair = [unpack(first, part, channels), unpack(second, part, channels)]
            spread(every, part * rows, jnp.concatenate(pair, axis=1))

    for b in range(step_bins):
        pick = pl.ds(step * step_bins + b, 2 * windows, stride=local_bins)
        here = [mine[t, pick, :] for t in range(mine.shape[0])]
        here = jnp.concatenate(here, axis=1)[:, :channels]
        left = here.astype(jnp.bfloat16)
        swapped = jnp.concatenate([here[windows:], -here[:windows]], axis=0).astype(jnp.bfloat16)
        right = [every[t, pick, :].astype(jnp.bfloat16) for t in range(every.shape[0])]
        right = jnp.concatenate(right, axis=1)[:, :width]
        for part, side in ((0, left), (1, swapped)):
            product = lax.dot_general(
                side, right, (((0,), (0,)), ((), ())), preferred_element_type=jnp.float32
            )
            out_ref[part, b] = (product * scale).astype(jnp.bfloat16)


def cross(own, other):
    windows, local_bins, width = own.shape
    channels = width // 2
    rows = 2 * windows * local_bins
    step_bins = 2 if local_bins % 2 == 0 else 1
    shape = (2, local_bins, channels, width)
    whole = pl.BlockSpec(memory_space=pltpu.VMEM)
    return pl.pallas_call(
        functools.partial(cross_kernel, 1.0 / windows),
        grid=(local_bins // step_bins,),
        out_shape=jax.ShapeDtypeStruct(shape, jnp.bfloat16),
        in_specs=[whole, whole],
        out_specs=pl.BlockSpec((2, step_bins, channels, width), lambda k: (0, k, 0, 0)),
        scratch_shapes=[
            pltpu.VMEM((pl.cdiv(channels, LANES), rows, LANES), jnp.float32),
            pltpu.VMEM((pl.cdiv(width, LANES), rows, LANES), jnp.float32),
        ],
        compiler_params=pltpu.CompilerParams(vmem_limit_bytes=50 << 20),
        cost_estimate=pl.CostEstimate(
            flops=2 * rows * channels * width * 2,
            bytes_accessed=2 * math.prod(shape),
            transcendentals=0,
        ),
        name="cross",
    )(own, other)


def local(samples):
    length = samples.shape[2]
    table = bin_table(length, BINS)
    spec = jnp.einsum("cws,sj->wcj", samples, table, preferred_element_type=jnp.float32)
    own, other = exchange(spec.astype(jnp.bfloat16), lax.axis_size("freq"))
    return jnp.swapaxes(cross(own, other), 2, 3)


def solution(mesh):
    return jax.shard_map(
        local,
        mesh=mesh,
        in_specs=(P("chan", ("hours", "freq"), None),),
        out_specs=P(None, ("hours", "freq"), None, "chan"),
        check_vma=False,
    )
```

```python
import functools
import math

import jax
import jax.numpy as jnp
import numpy as np
from jax import lax
from jax.experimental import pallas as pl
from jax.experimental.pallas import tpu as pltpu
from jax.sharding import PartitionSpec as P

BINS = 128
LANES = 128
MESH = pl.DeviceIdType.MESH


def bin_table(length, bins):
    position = np.arange(length, dtype=np.int64)[:, None]
    number = np.arange(bins, dtype=np.int64)[None, :] + 1
    step = np.float32(2.0 * math.pi / length)
    phase = (position * number % length).astype(np.float32) * step
    half = np.float32(0.5)
    taper = half - half * np.cos(position.astype(np.float32) * step)
    factor = np.float32(math.sqrt(8.0 / (3.0 * length)))
    table = np.concatenate([taper * np.cos(phase), -(taper * np.sin(phase))], axis=1) * factor
    return jnp.asarray(table.astype(np.float32)).astype(jnp.bfloat16)


def whiten(real, imag):
    bins = real.shape[0]
    power = real * real + imag * imag
    row = lax.broadcasted_iota(jnp.int32, (bins, 1), 0)
    summed = power
    for shift in (1, 2):
        summed = summed + jnp.where(row >= shift, pltpu.roll(power, shift, 0), 0.0)
        summed = summed + jnp.where(row < bins - shift, pltpu.roll(power, bins - shift, 0), 0.0)
    count = jnp.minimum(row + 2, bins - 1) - jnp.maximum(row - 2, 0) + 1
    level = jnp.maximum(summed * (1.0 / count.astype(jnp.float32)), 0.1)
    scale = lax.rsqrt(level)
    return real * scale, imag * scale


def pack(real, imag):
    cut = real.shape[1] // LANES * LANES
    return jnp.concatenate([real[:, :cut], imag[:, :cut], real[:, cut:], imag[:, cut:]], axis=1)


def unpack(values, part, channels):
    cut = channels // LANES * LANES
    rest = channels - cut
    tail = 2 * cut + part * rest
    main = values[:, part * cut : (part + 1) * cut]
    return jnp.concatenate([main, values[:, tail : tail + rest]], axis=1) if rest else main


def exchange_kernel(count, spec_ref, own_ref, other_ref, white, send_sem, recv_sem, local_sem,
                    pass_sem, got_sem):
    hour = lax.axis_index("hours")
    chan = lax.axis_index("chan")
    me = lax.axis_index("freq")
    windows = spec_ref.shape[0]
    local_bins, width = own_ref.shape[1:]
    steps = sorted(range(1, count), key=lambda step: abs(2 * step - count))

    barrier = pltpu.get_barrier_semaphore()
    for step in steps:
        peer = lax.rem(me + step, count)
        pl.semaphore_signal(barrier, inc=1, device_id=(hour, chan, peer), device_id_type=MESH)
    pl.semaphore_signal(barrier, inc=1, device_id=(hour, 1 - chan, me), device_id_type=MESH)

    copies, passes = {}, []

    def block(owner):
        return own_ref.at[pl.ds(windows * owner, windows)]

    def forward(source_ref, owner, step):
        copy = pltpu.make_async_remote_copy(
            src_ref=source_ref,
            dst_ref=other_ref.at[pl.ds(windows * owner, windows)],
            send_sem=pass_sem.at[step],
            recv_sem=got_sem.at[step],
            device_id=(hour, 1 - chan, me),
            device_id_type=MESH,
        )
        copy.start()
        passes.append(copy)

    for w in range(windows):
        turned = spec_ref[w].T.astype(jnp.float32)
        real, imag = whiten(turned[:BINS], turned[BINS:])
        packed = pack(real, imag).astype(jnp.bfloat16)
        white[:, w] = packed.reshape(count, local_bins, width)
    pl.semaphore_wait(barrier, count)
    for step in steps:
        peer = lax.rem(me + step, count)
        copies[step] = pltpu.make_async_remote_copy(
            src_ref=white.at[peer],
            dst_ref=block(me),
            send_sem=send_sem.at[step],
            recv_sem=recv_sem.at[step],
            device_id=(hour, chan, peer),
            device_id_type=MESH,
        )
        copies[step].start()
    keep = pltpu.make_async_copy(white.at[me], block(me), local_sem)
    keep.start()
    forward(white.at[me], me, 0)
    for step in reversed(steps):
        copies[step].wait_recv()
        owner = lax.rem(me - step + count, count)
        forward(block(owner), owner, step)
    keep.wait()
    for copy in copies.values():
        copy.wait_send()
    for copy in passes:
        copy.wait()


def exchange(spec, count):
    windows, channels, _ = spec.shape
    local_bins = BINS // count
    shape = jax.ShapeDtypeStruct((windows * count, local_bins, 2 * channels), jnp.bfloat16)
    pieces = pltpu.SemaphoreType.DMA((count,))
    return pl.pallas_call(
        functools.partial(exchange_kernel, count),
        out_shape=(shape, shape),
        in_specs=[pl.BlockSpec(memory_space=pltpu.VMEM)],
        out_specs=(pl.BlockSpec(memory_space=pl.ANY), pl.BlockSpec(memory_space=pl.ANY)),
        scratch_shapes=[
            pltpu.VMEM((count, windows, local_bins, 2 * channels), jnp.bfloat16),
            pieces,
            pieces,
            pltpu.SemaphoreType.DMA,
            pieces,
            pieces,
        ],
        compiler_params=pltpu.CompilerParams(
            collective_id=0, has_side_effects=True, vmem_limit_bytes=40 << 20
        ),
        cost_estimate=pl.CostEstimate(
            flops=spec.size * 20, bytes_accessed=spec.size * 8, transcendentals=0
        ),
        name="exchange",
    )(spec)


def spread(tiles, first_row, values):
    height, width = values.shape
    for t in range(tiles.shape[0]):
        part = values[:, t * LANES : min((t + 1) * LANES, width)]
        if part.shape[1] < LANES:
            gap = jnp.zeros((height, LANES - part.shape[1]), part.dtype)
            part = jnp.concatenate([part, gap], axis=1)
        tiles[t, first_row : first_row + height] = part


def cross_kernel(scale, own_ref, other_ref, out_ref, mine, every):
    chan = lax.axis_index("chan")
    windows, local_bins, width = own_ref.shape
    channels = width // 2
    rows = windows * local_bins
    step_bins = out_ref.shape[1]
    step = pl.program_id(0)

    @pl.when(step == 0)
    def _():
        own = own_ref[...].astype(jnp.float32).reshape(rows, width)
        other = other_ref[...].astype(jnp.float32).reshape(rows, width)
        first = jnp.where(chan == 0, own, other)
        second = jnp.where(chan == 0, other, own)
        for part in range(2):
            spread(mine, part * rows, unpack(own, part, channels))
            pair = [unpack(first, part, channels), unpack(second, part, channels)]
            spread(every, part * rows, jnp.concatenate(pair, axis=1))

    for b in range(step_bins):
        pick = pl.ds(step * step_bins + b, 2 * windows, stride=local_bins)
        here = [mine[t, pick, :] for t in range(mine.shape[0])]
        here = jnp.concatenate(here, axis=1)[:, :channels]
        left = here.astype(jnp.bfloat16)
        swapped = jnp.concatenate([here[windows:], -here[:windows]], axis=0).astype(jnp.bfloat16)
        right = [every[t, pick, :].astype(jnp.bfloat16) for t in range(every.shape[0])]
        right = jnp.concatenate(right, axis=1)[:, :width]
        for part, side in ((0, left), (1, swapped)):
            product = lax.dot_general(
                side, right, (((0,), (0,)), ((), ())), preferred_element_type=jnp.float32
            )
            out_ref[part, b] = (product * scale).astype(jnp.bfloat16)


def cross(own, other):
    windows, local_bins, width = own.shape
    channels = width // 2
    rows = 2 * windows * local_bins
    step_bins = 2 if local_bins % 2 == 0 else 1
    shape = (2, local_bins, channels, width)
    whole = pl.BlockSpec(memory_space=pltpu.VMEM)
    return pl.pallas_call(
        functools.partial(cross_kernel, 1.0 / windows),
        grid=(local_bins // step_bins,),
        out_shape=jax.ShapeDtypeStruct(shape, jnp.bfloat16),
        in_specs=[whole, whole],
        out_specs=pl.BlockSpec((2, step_bins, channels, width), lambda k: (0, k, 0, 0)),
        scratch_shapes=[
            pltpu.VMEM((pl.cdiv(channels, LANES), rows, LANES), jnp.float32),
            pltpu.VMEM((pl.cdiv(width, LANES), rows, LANES), jnp.float32),
        ],
        compiler_params=pltpu.CompilerParams(vmem_limit_bytes=50 << 20),
        cost_estimate=pl.CostEstimate(
            flops=2 * rows * channels * width * 2,
            bytes_accessed=2 * math.prod(shape),
            transcendentals=0,
        ),
        name="cross",
    )(own, other)


def local(samples):
    length = samples.shape[2]
    table = bin_table(length, BINS)
    spec = jnp.einsum("cws,sj->wcj", samples, table, preferred_element_type=jnp.float32)
    own, other = exchange(spec.astype(jnp.bfloat16), lax.axis_size("freq"))
    return jnp.swapaxes(cross(own, other), 2, 3)


def solution(mesh):
    return jax.shard_map(
        local,
        mesh=mesh,
        in_specs=(P("chan", ("hours", "freq"), None),),
        out_specs=P(None, ("hours", "freq"), None, "chan"),
        check_vma=False,
    )
```
